32 devices in a mesh: parts: 2 (over x), seq: 16 (over z, y, core).
Axes of the slice: x: 2, y: 2, z: 4, core: 2. Of those that a mesh axis runs over, the one named last changes fastest.
Arguments:
- queries: bfloat16 [4096, 1024], P(('parts', 'seq')), parts along dimension 0, may hold values from -6 to 6
- keys: bfloat16 [4096, 1024], P(('parts', 'seq')), parts along dimension 0, may hold values from -6 to 6
- values: bfloat16 [4096, 1024], P(('parts', 'seq')), parts along dimension 0, may hold values from -6 to 6
- out_grads: bfloat16 [4096, 1024], P(('parts', 'seq')), parts along dimension 0, may hold values from -6 to 6
Outputs:
- query_out: bfloat16 [4096, 1024], P(('parts', 'seq')), parts along dimension 0
- key_out: bfloat16 [4096, 1024], P(('parts', 'seq')), parts along dimension 0
- value_out: bfloat16 [4096, 1024], P(('parts', 'seq')), parts along dimension 0
The draws below stay inside these ranges and needn't reach their ends.
There are 2 independent parts, one for each index of `parts`. The reference program is written for one: setup_inputs(seed, part) draws one part's arguments, and reference() takes and returns one part's arrays. A program takes and returns all parts, laid end to end along the dimension named above; each array names one. Nothing has to cross between parts.
All inputs are finite; a program needn't handle non-finite values.
Results may differ from the reference program's by a relative error of at most 0.0049.
Values sent between devices are 32-bit elements; how exact they have to be, the bound alone decides.
No kernel may reach another device: no remote copies, remote signals or barrier semaphores. Data moves between devices by JAX's collectives and lax.ppermute only.
A program may use at most 192 MiB of HBM per device.

```python
import math
import jax
import jax.numpy as jnp
from jax import lax

HEADS = 8
HEAD_DIM = 128
GROUP = 128
TOKENS = 2048


def steps_of(own_key, dims, cuts, low, largest):
    gain = 1.0
    for dim, shards_of in cuts:
        steps = jax.random.uniform(jax.random.fold_in(jax.random.fold_in(own_key, 6), dim), (shards_of,), jnp.float32, low / len(cuts), largest / len(cuts))
        gain = gain * jnp.repeat(jnp.exp(steps), dims[dim] // shards_of).reshape((-1,) + (1,) * (len(dims) - 1 - dim))
    return gain


def normal_values(key, extent, deviation, reach, pieces=(), dtype=jnp.bfloat16):
    drawn = jax.random.normal(key, extent, jnp.float32) * deviation
    if len(pieces) > 0:
        drawn = steps_of(key, extent, pieces, -0.22, 0.18) * drawn
    return jnp.clip(drawn, min=-reach, max=reach).astype(dtype)


def setup_inputs(seed: int = 0, part: int = 0) -> dict:
    streams_of = jax.random.split(jax.random.key(seed), 5)
    own_keys = jax.random.split(jax.random.fold_in(streams_of[4], part), 5)
    queries = normal_values(own_keys[0], (TOKENS, HEADS * HEAD_DIM), 1.0, 6.0, ((0, 16),))
    keys = normal_values(own_keys[1], (TOKENS, HEADS * HEAD_DIM), 1.0, 6.0, ((0, 16),))
    values = normal_values(own_keys[2], (TOKENS, HEADS * HEAD_DIM), 1.0, 6.0, ((0, 16),))
    out_grads = normal_values(own_keys[3], (TOKENS, HEADS * HEAD_DIM), 1.0, 6.0, ((0, 16),))
    return dict(queries=queries, keys=keys, values=values, out_grads=out_grads)


def blocked(array, group_count):
    return array.reshape(group_count, GROUP, HEADS, HEAD_DIM).astype(jnp.float32)

def rounded(array):
    return lax.optimization_barrier(array.astype(jnp.bfloat16)).astype(jnp.float32)

def reference(queries, keys, values, out_grads):
    group_count = TOKENS // GROUP
    factor = 1.0 / math.sqrt(HEAD_DIM * TOKENS)
    query_f = blocked(queries, group_count)
    key_f = blocked(keys, group_count)
    value_f = blocked(values, group_count)
    grad_f = blocked(out_grads, group_count)
    key_value = jnp.einsum('ncha,nchb->nhab', key_f, value_f)
    query_grad = jnp.einsum('ncha,nchb->nhab', query_f, grad_f)
    empty_state = jnp.zeros((1, HEADS, HEAD_DIM, HEAD_DIM), jnp.float32)
    earlier = jnp.concatenate([empty_state, jnp.cumsum(key_value, 0)[:-1]], 0)
    future = jnp.concatenate([jnp.cumsum(query_grad[::-1], 0)[::-1][1:], empty_state], 0)
    earlier = rounded(earlier)
    future = rounded(future)
    positions = jnp.arange(GROUP)
    causal = (positions[None, :] <= positions[:, None]).astype(jnp.float32)
    scores = rounded(jnp.einsum('ncha,nsha->nhcs', query_f, key_f) * causal)
    grad_scores = rounded(jnp.einsum('nchb,nshb->nhcs', grad_f, value_f) * causal)
    query_out = jnp.einsum('nhcs,nsha->ncha', grad_scores, key_f) + jnp.einsum('nchb,nhab->ncha', grad_f, earlier)
    key_out = jnp.einsum('nhcs,ncha->nsha', grad_scores, query_f) + jnp.einsum('nshb,nhab->nsha', value_f, future)
    value_out = jnp.einsum('nhcs,nchb->nshb', scores, grad_f) + jnp.einsum('nsha,nhab->nshb', key_f, future)

    def finish(array):
        return (factor * array).reshape(TOKENS, HEADS * HEAD_DIM).astype(jnp.bfloat16)
    return (finish(query_out), finish(key_out), finish(value_out))
```

```python
import math

import jax
import jax.numpy as jnp
from jax import lax
from jax.experimental import pallas as pl
from jax.experimental.pallas import tpu as pltpu
from jax.sharding import PartitionSpec as P

HEADS = 8
HEAD_DIM = 128
GROUP = 128
AXIS = "seq"
VMEM = pl.BlockSpec(memory_space=pltpu.VMEM)


def place():
    index = lax.axis_index(AXIS)
    square = index >> 3
    return index & 1, (index >> 1) & 3, square, (square & 1) == 0


def swap(x, mask):
    count = lax.axis_size(AXIS)
    return lax.ppermute(x, AXIS, [(i, i ^ mask) for i in range(count)])


def columns(head):
    return pl.ds(pl.multiple_of(head * HEAD_DIM, HEAD_DIM), HEAD_DIM)


def dot(a, b, dims):
    return lax.dot_general(a, b, (dims, ((), ())), preferred_element_type=jnp.float32)


def states_kernel(first, q_ref, k_ref, v_ref, g_ref, keep_ref, send_ref):
    core, chip, _, even = place()
    pick = even if first else jnp.logical_not(even)

    def run(x_ref, y_ref):
        for half, out in ((1, send_ref), (0, keep_ref)):
            for slot in range(4):
                cols = columns(4 * (core ^ half) + (chip ^ slot))
                out[slot] = dot(x_ref[:, cols], y_ref[:, cols], ((0,), (0,)))

    pl.when(pick)(lambda: run(k_ref, v_ref))
    pl.when(jnp.logical_not(pick))(lambda: run(q_ref, g_ref))


def states(first, args):
    out = jax.ShapeDtypeStruct((4, HEAD_DIM, HEAD_DIM), jnp.float32)
    return pl.pallas_call(
        lambda *refs: states_kernel(first, *refs),
        out_shape=(out, out),
        in_specs=[VMEM] * 4,
        out_specs=(VMEM, VMEM),
        cost_estimate=pl.CostEstimate(flops=2 * 8 * 128**3, bytes_accessed=2**20, transcendentals=0),
        name="states",
    )(*args)


def inner_kernel(q_ref, k_ref, v_ref, g_ref, qo_ref, ko_ref, vo_ref):
    row = lax.broadcasted_iota(jnp.int32, (GROUP, GROUP), 0)
    col = lax.broadcasted_iota(jnp.int32, (GROUP, GROUP), 1)
    causal = col <= row
    for head in range(HEADS):
        cols = slice(head * HEAD_DIM, (head + 1) * HEAD_DIM)
        q, k, v, g = q_ref[:, cols], k_ref[:, cols], v_ref[:, cols], g_ref[:, cols]
        scores = jnp.where(causal, dot(q, k, ((1,), (1,))), 0.0).astype(jnp.bfloat16)
        grads = jnp.where(causal, dot(g, v, ((1,), (1,))), 0.0).astype(jnp.bfloat16)
        qo_ref[:, cols] = dot(grads, k, ((1,), (0,)))
        ko_ref[:, cols] = dot(grads, q, ((0,), (0,)))
        vo_ref[:, cols] = dot(scores, g, ((0,), (0,)))


def inner(args):
    out = jax.ShapeDtypeStruct(args[0].shape, jnp.float32)
    return pl.pallas_call(
        inner_kernel,
        out_shape=(out, out, out),
        in_specs=[VMEM] * 4,
        out_specs=(VMEM,) * 3,
        cost_estimate=pl.CostEstimate(flops=5 * 2 * 8 * 128**3, bytes_accessed=2**20, transcendentals=0),
        name="inner",
    )(*args)


def final_kernel(factor, k_ref, v_ref, g_ref, qi_ref, ki_ref, vi_ref, *refs):
    blocks, (qo_ref, ko_ref, vo_ref) = refs[:4], refs[4:]
    core, chip, _, even = place()
    own_a, own_b, other_a, other_b = blocks

    def run(flip):
        for half, a_ref, b_ref in ((0, own_a, own_b), (1, other_a, other_b)):
            earlier_ref, future_ref = (b_ref, a_ref) if flip else (a_ref, b_ref)
            for slot in range(4):
                cols = columns(4 * (core ^ half) + (chip ^ slot))
                earlier = earlier_ref[slot].astype(jnp.bfloat16)
                future = future_ref[slot].astype(jnp.bfloat16)
                qo = qi_ref[:, cols] + dot(g_ref[:, cols], earlier, ((1,), (1,)))
                ko = ki_ref[:, cols] + dot(v_ref[:, cols], future, ((1,), (1,)))
                vo = vi_ref[:, cols] + dot(k_ref[:, cols], future, ((1,), (0,)))
                qo_ref[:, cols] = (factor * qo).astype(jnp.bfloat16)
                ko_ref[:, cols] = (factor * ko).astype(jnp.bfloat16)
                vo_ref[:, cols] = (factor * vo).astype(jnp.bfloat16)

    pl.when(even)(lambda: run(False))
    pl.when(jnp.logical_not(even))(lambda: run(True))


def final(factor, *args):
    out = jax.ShapeDtypeStruct(args[0].shape, jnp.bfloat16)
    return pl.pallas_call(
        lambda *refs: final_kernel(factor, *refs),
        out_shape=(out, out, out),
        in_specs=[VMEM] * len(args),
        out_specs=(VMEM,) * 3,
        name="final",
    )(*args)


def scan(parts, chip, forward):
    sums = []
    for m in range(4):
        total = None
        for k in range(4):
            if k != m:
                ahead = jnp.where(forward, (chip ^ k) < (chip ^ m), (chip ^ k) > (chip ^ m))
                part = jnp.where(ahead, parts[k], 0.0)
                total = part if total is None else total + part
        sums.append(total)
    return sums


def between_squares(sum_a, sum_b, square, even, squares):
    if squares == 2:
        return None, swap(sum_a, 8)
    kv, qg = jnp.where(even, sum_a, sum_b), jnp.where(even, sum_b, sum_a)
    before, after = jnp.zeros_like(kv), jnp.zeros_like(qg)
    half = 1
    while half < squares:
        upper = (square & half) != 0
        out = jnp.where(upper, after + qg, before + kv)
        got = jnp.zeros_like(out)
        for step in range(half):
            pairs = []
            for base in range(0, squares, 2 * half):
                low, high = base + half - 1, base + half
                for r in range(8):
                    pairs.append((8 * low + r, 8 * (high + step) + r))
                    pairs.append((8 * high + r, 8 * (low - step) + r))
            got = got + lax.ppermute(out, AXIS, pairs)
        before, after = jnp.where(upper, before + got, before), jnp.where(upper, after, after + got)
        half *= 2
    return jnp.where(even, before, after), jnp.where(even, after, before)


def local(*args):
    queries, keys, values, out_grads = args
    devices = lax.axis_size(AXIS)
    factor = 1.0 / math.sqrt(HEAD_DIM * queries.shape[0] * devices)
    core, chip, square, even = place()

    keep_a, send_a = states(True, args)
    got_a = swap(send_a, 1)
    keep_b, send_b = states(False, args)
    got_b = swap(send_b, 1)
    total_a, total_b = keep_a + got_a, keep_b + got_b

    parts_a, parts_b = [total_a[0]], [total_b[0]]
    for m in (1, 2, 3):
        parts_a.append(swap(total_a[m], 2 * m))
    for m in (1, 2, 3):
        parts_b.append(swap(total_b[m], 2 * m))
    ahead_a, ahead_b = between_squares(sum(parts_a[1:], parts_a[0]), sum(parts_b[1:], parts_b[0]), square, even, devices // 8)
    scan_a, scan_b = scan(parts_a, chip, even), scan(parts_b, chip, jnp.logical_not(even))
    if ahead_a is not None:
        scan_a = [s + ahead_a for s in scan_a]
    scan_b = [s + ahead_b for s in scan_b]

    both = [jnp.stack([a, b]) for a, b in zip(scan_a, scan_b)]
    back = [both[0]] + [swap(both[m], 2 * m) for m in (1, 2, 3)]
    chip_a = jnp.stack([x[0] for x in back])
    chip_b = jnp.stack([x[1] for x in back])
    last = (core == 1) == even
    own_a, own_b = jnp.where(last, chip_a + got_a, chip_a), jnp.where(last, chip_b, chip_b + got_b)
    pair_a, pair_b = jnp.where(last, chip_a, chip_a + keep_a), jnp.where(last, chip_b + keep_b, chip_b)
    other = swap(jnp.stack([pair_a, pair_b]), 1)

    inner_q, inner_k, inner_v = inner(args)
    return final(factor, keys, values, out_grads, inner_q, inner_k, inner_v, own_a, own_b, other[0], other[1])


def solution(mesh):
    spec = P(("parts", "seq"), None)
    return jax.shard_map(local, mesh=mesh, in_specs=(spec,) * 4, out_specs=(spec,) * 3, check_vma=False)
```

```python
import math

import jax
import jax.numpy as jnp
from jax import lax
from jax.experimental import pallas as pl
from jax.experimental.pallas import tpu as pltpu
from jax.sharding import PartitionSpec as P

HEADS = 8
HEAD_DIM = 128
GROUP = 128
AXIS = "seq"
VMEM = pl.BlockSpec(memory_space=pltpu.VMEM)
HBM = pl.BlockSpec(memory_space=pltpu.HBM)
PARAMS = pltpu.CompilerParams(vmem_limit_bytes=16 * 2**20)


def place():
    index = lax.axis_index(AXIS)
    square = index >> 3
    return index & 1, (index >> 1) & 3, square, (square & 1) == 0


def swap(x, mask):
    count = lax.axis_size(AXIS)
    return lax.ppermute(x, AXIS, [(i, i ^ mask) for i in range(count)])


def columns(head):
    return pl.ds(pl.multiple_of(head * HEAD_DIM, HEAD_DIM), HEAD_DIM)


def dot(a, b, dims):
    return lax.dot_general(a, b, (dims, ((), ())), preferred_element_type=jnp.float32)


def states_kernel(q_hbm, k_hbm, v_hbm, g_hbm, q_ref, k_ref, v_ref, g_ref, keep_a, send_a, keep_b, send_b, sems):
    core, chip, _, even = place()
    pairs = ((q_hbm, q_ref), (k_hbm, k_ref), (v_hbm, v_ref), (g_hbm, g_ref))
    loads = [pltpu.make_async_copy(src, dst, sems.at[i]) for i, (src, dst) in enumerate(pairs)]
    for load in loads:
        load.start()
    for load in loads:
        load.wait()

    def run(x_ref, y_ref, keep_ref, send_ref):
        for half, out in ((1, send_ref), (0, keep_ref)):
            for slot in range(4):
                cols = columns(4 * (core ^ half) + (chip ^ slot))
                out[slot] = dot(x_ref[:, cols], y_ref[:, cols], ((0,), (0,)))

    @pl.when(even)
    def _():
        run(k_ref, v_ref, keep_a, send_a)
        run(q_ref, g_ref, keep_b, send_b)

    @pl.when(jnp.logical_not(even))
    def _():
        run(q_ref, g_ref, keep_a, send_a)
        run(k_ref, v_ref, keep_b, send_b)


def states(args):
    rows = jax.ShapeDtypeStruct(args[0].shape, args[0].dtype)
    out = jax.ShapeDtypeStruct((4, HEAD_DIM, HEAD_DIM), jnp.float32)
    return pl.pallas_call(
        states_kernel,
        out_shape=(rows,) * 4 + (out,) * 4,
        in_specs=[HBM] * 4,
        out_specs=(VMEM,) * 8,
        scratch_shapes=[pltpu.SemaphoreType.DMA((4,))],
        compiler_params=PARAMS,
        name="states",
    )(*(pltpu.with_memory_space_constraint(x, pltpu.HBM) for x in args))


def inner_kernel(q_ref, k_ref, v_ref, g_ref, qo_ref, ko_ref, vo_ref):
    row = lax.broadcasted_iota(jnp.int32, (GROUP, GROUP), 0)
    col = lax.broadcasted_iota(jnp.int32, (GROUP, GROUP), 1)
    causal = col <= row
    for head in range(HEADS):
        cols = slice(head * HEAD_DIM, (head + 1) * HEAD_DIM)
        q, k, v, g = q_ref[:, cols], k_ref[:, cols], v_ref[:, cols], g_ref[:, cols]
        scores = jnp.where(causal, dot(q, k, ((1,), (1,))), 0.0).astype(jnp.bfloat16)
        grads = jnp.where(causal, dot(g, v, ((1,), (1,))), 0.0).astype(jnp.bfloat16)
        qo_ref[:, cols] = dot(grads, k, ((1,), (0,)))
        ko_ref[:, cols] = dot(grads, q, ((0,), (0,)))
        vo_ref[:, cols] = dot(scores, g, ((0,), (0,)))


def inner(args):
    out = jax.ShapeDtypeStruct(args[0].shape, jnp.float32)
    return pl.pallas_call(
        inner_kernel,
        out_shape=(out, out, out),
        in_specs=[VMEM] * 4,
        out_specs=(VMEM,) * 3,
        cost_estimate=pl.CostEstimate(flops=5 * 2 * 8 * 128**3, bytes_accessed=2**20, transcendentals=0),
        compiler_params=PARAMS,
        name="inner",
    )(*args)


def final_kernel(factor, half, k_ref, v_ref, g_ref, qi_ref, ki_ref, vi_ref, a_ref, b_ref, *refs):
    qo_hbm, ko_hbm, vo_hbm, buffer, sems = refs[-5:]
    core, chip, _, even = place()

    def run(earlier_ref, future_ref):
        for slot in range(4):
            cols = columns(4 * (core ^ half) + (chip ^ slot))
            earlier = earlier_ref[slot].astype(jnp.bfloat16)
            future = future_ref[slot].astype(jnp.bfloat16)
            qo = qi_ref[:, cols] + dot(g_ref[:, cols], earlier, ((1,), (1,)))
            ko = ki_ref[:, cols] + dot(v_ref[:, cols], future, ((1,), (1,)))
            vo = vi_ref[:, cols] + dot(k_ref[:, cols], future, ((1,), (0,)))
            for i, value in enumerate((qo, ko, vo)):
                buffer[i, slot] = (factor * value).astype(jnp.bfloat16)

    pl.when(even)(lambda: run(a_ref, b_ref))
    pl.when(jnp.logical_not(even))(lambda: run(b_ref, a_ref))
    stores = []
    for slot in range(4):
        cols = columns(4 * (core ^ half) + (chip ^ slot))
        for i, out in enumerate((qo_hbm, ko_hbm, vo_hbm)):
            stores.append(pltpu.make_async_copy(buffer.at[i, slot], out.at[:, cols], sems.at[i, slot]))
            stores[-1].start()
    for store in stores:
        store.wait()


def final(factor, half, inputs, outs=()):
    out = jax.ShapeDtypeStruct(inputs[0].shape, jnp.bfloat16)
    return pl.pallas_call(
        lambda *refs: final_kernel(factor, half, *refs),
        out_shape=(out, out, out),
        in_specs=[VMEM] * len(inputs) + [HBM] * len(outs),
        out_specs=(HBM,) * 3,
        scratch_shapes=[pltpu.VMEM((3, 4, GROUP, HEAD_DIM), jnp.bfloat16), pltpu.SemaphoreType.DMA((3, 4))],
        input_output_aliases={len(inputs) + i: i for i in range(len(outs))},
        compiler_params=PARAMS,
        name="final",
    )(*inputs, *outs)


def scan(parts, chip, forward):
    sums = []
    for m in range(4):
        total = None
        for k in range(4):
            if k != m:
                ahead = jnp.where(forward, (chip ^ k) < (chip ^ m), (chip ^ k) > (chip ^ m))
                part = jnp.where(ahead, parts[k], 0.0)
                total = part if total is None else total + part
        sums.append(total)
    return sums


def between_squares(sum_a, sum_b, square, even, squares):
    if squares == 2:
        return None, swap(sum_a, 8)
    kv, qg = jnp.where(even, sum_a, sum_b), jnp.where(even, sum_b, sum_a)
    before, after = jnp.zeros_like(kv), jnp.zeros_like(qg)
    half = 1
    while half < squares:
        upper = (square & half) != 0
        out = jnp.where(upper, after + qg, before + kv)
        got = jnp.zeros_like(out)
        for step in range(half):
            pairs = []
            for base in range(0, squares, 2 * half):
                low, high = base + half - 1, base + half
                for r in range(8):
                    pairs.append((8 * low + r, 8 * (high + step) + r))
                    pairs.append((8 * high + r, 8 * (low - step) + r))
            got = got + lax.ppermute(out, AXIS, pairs)
        before, after = jnp.where(upper, before + got, before), jnp.where(upper, after, after + got)
        half *= 2
    return jnp.where(even, before, after), jnp.where(even, after, before)


def local(*args):
    queries, keys, values, out_grads = args
    devices = lax.axis_size(AXIS)
    factor = 1.0 / math.sqrt(HEAD_DIM * queries.shape[0] * devices)
    core, chip, square, even = place()

    *args, keep_a, send_a, keep_b, send_b = states(args)
    _, keys, values, out_grads = args
    got_a = swap(send_a, 1)
    got_b = swap(send_b, 1)
    own_part = inner(args)
    total_a, total_b = keep_a + got_a, keep_b + got_b

    parts_a, parts_b = [total_a[0]], [total_b[0]]
    for m in (1, 2, 3):
        parts_a.append(swap(total_a[m], 2 * m))
    for m in (1, 2, 3):
        parts_b.append(swap(total_b[m], 2 * m))
    ahead_a, ahead_b = between_squares(sum(parts_a[1:], parts_a[0]), sum(parts_b[1:], parts_b[0]), square, even, devices // 8)
    scan_a, scan_b = scan(parts_a, chip, even), scan(parts_b, chip, jnp.logical_not(even))
    if ahead_a is not None:
        scan_a = [s + ahead_a for s in scan_a]
    scan_b = [s + ahead_b for s in scan_b]

    both = [jnp.stack([a, b]) for a, b in zip(scan_a, scan_b)]
    back = [both[0]] + [swap(both[m], 2 * m) for m in (1, 2, 3)]
    back[3], own_part = lax.optimization_barrier((back[3], own_part))
    chip_a = jnp.stack([x[0] for x in back])
    chip_b = jnp.stack([x[1] for x in back])
    last = (core == 1) == even
    own_a, own_b = jnp.where(last, chip_a + got_a, chip_a), jnp.where(last, chip_b, chip_b + got_b)
    pair_a, pair_b = jnp.where(last, chip_a, chip_a + keep_a), jnp.where(last, chip_b + keep_b, chip_b)
    other = swap(jnp.stack([pair_a, pair_b]), 1)

    inputs = (keys, values, out_grads, *own_part)
    outs = final(factor, 0, (*inputs, own_a, own_b))
    return final(factor, 1, (*inputs, other[0], other[1]), outs)


def solution(mesh):
    spec = P(("parts", "seq"), None)
    return jax.shard_map(local, mesh=mesh, in_specs=(spec,) * 4, out_specs=(spec,) * 3, check_vma=False)
```

```python
import math

import jax
import jax.numpy as jnp
from jax import lax
from jax.experimental import pallas as pl
from jax.experimental.pallas import tpu as pltpu
from jax.sharding import PartitionSpec as P

HEADS = 8
HEAD_DIM = 128
GROUP = 128
AXIS = "seq"
VMEM = pl.BlockSpec(memory_space=pltpu.VMEM)
HBM = pl.BlockSpec(memory_space=pltpu.HBM)
PARAMS = pltpu.CompilerParams(vmem_limit_bytes=16 * 2**20)
PIECES = ((0, 3), (1, 2))


def place():
    index = lax.axis_index(AXIS)
    square = index >> 3
    return index & 1, (index >> 1) & 3, square, (square & 1) == 0


def swap(x, mask):
    count = lax.axis_size(AXIS)
    return lax.ppermute(x, AXIS, [(i, i ^ mask) for i in range(count)])


def columns(half, slot, core, chip):
    return pl.ds(pl.multiple_of((4 * (core ^ half) + (chip ^ slot)) * HEAD_DIM, HEAD_DIM), HEAD_DIM)


def dot(a, b, dims):
    return lax.dot_general(a, b, (dims, ((), ())), preferred_element_type=jnp.float32)


def heads(*count):
    return jax.ShapeDtypeStruct((*count, HEAD_DIM, HEAD_DIM), jnp.float32)


def in_vmem(kernel, out_shape, args, name):
    return pl.pallas_call(
        kernel,
        out_shape=out_shape,
        in_specs=[VMEM] * len(args),
        out_specs=jax.tree.map(lambda _: VMEM, out_shape),
        compiler_params=PARAMS,
        name=name,
    )(*args)


def write_states(x_ref, y_ref, out_ref, half, core, chip):
    for slot in range(4):
        cols = columns(half, slot, core, chip)
        out_ref[slot] = dot(x_ref[:, cols], y_ref[:, cols], ((0,), (0,)))


def first_kernel(q_hbm, k_hbm, v_hbm, g_hbm, q_ref, k_ref, v_ref, g_ref, send_ref, sems):
    core, chip, _, even = place()
    q, k, v, g = (
        pltpu.make_async_copy(src, dst, sems.at[i])
        for i, (src, dst) in enumerate(((q_hbm, q_ref), (k_hbm, k_ref), (v_hbm, v_ref), (g_hbm, g_ref)))
    )

    def run(now, later, x_ref, y_ref):
        for load in (*now, *later):
            load.start()
        for load in now:
            load.wait()
        write_states(x_ref, y_ref, send_ref, 1, core, chip)
        for load in later:
            load.wait()

    pl.when(even)(lambda: run((k, v), (q, g), k_ref, v_ref))
    pl.when(jnp.logical_not(even))(lambda: run((q, g), (k, v), q_ref, g_ref))


def first_states(args):
    rows = jax.ShapeDtypeStruct(args[0].shape, args[0].dtype)
    return pl.pallas_call(
        first_kernel,
        out_shape=(rows,) * 4 + (heads(4),),
        in_specs=[HBM] * 4,
        out_specs=(VMEM,) * 5,
        scratch_shapes=[pltpu.SemaphoreType.DMA((4,))],
        compiler_params=PARAMS,
        name="first_states",
    )(*(pltpu.with_memory_space_constraint(x, pltpu.HBM) for x in args))


def second_kernel(q_ref, k_ref, v_ref, g_ref, send_b, keep_a, keep_b):
    core, chip, _, even = place()

    def run(x_ref, y_ref, z_ref, w_ref):
        write_states(z_ref, w_ref, send_b, 1, core, chip)
        write_states(x_ref, y_ref, keep_a, 0, core, chip)
        write_states(z_ref, w_ref, keep_b, 0, core, chip)

    pl.when(even)(lambda: run(k_ref, v_ref, q_ref, g_ref))
    pl.when(jnp.logical_not(even))(lambda: run(q_ref, g_ref, k_ref, v_ref))


def inner_kernel(q_ref, k_ref, v_ref, g_ref, qo_ref, ko_ref, vo_ref):
    row = lax.broadcasted_iota(jnp.int32, (GROUP, GROUP), 0)
    col = lax.broadcasted_iota(jnp.int32, (GROUP, GROUP), 1)
    causal = col <= row
    for head in range(HEADS):
        cols = slice(head * HEAD_DIM, (head + 1) * HEAD_DIM)
        q, k, v, g = q_ref[:, cols], k_ref[:, cols], v_ref[:, cols], g_ref[:, cols]
        scores = jnp.where(causal, dot(q, k, ((1,), (1,))), 0.0).astype(jnp.bfloat16)
        grads = jnp.where(causal, dot(g, v, ((1,), (1,))), 0.0).astype(jnp.bfloat16)
        qo_ref[:, cols] = dot(grads, k, ((1,), (0,)))
        ko_ref[:, cols] = dot(grads, q, ((0,), (0,)))
        vo_ref[:, cols] = dot(scores, g, ((0,), (0,)))


def scan(parts, start, slot, chip, forward):
    total = start
    for k in range(4):
        if k != slot:
            use = jnp.where(forward, (chip ^ k) < (chip ^ slot), (chip ^ k) > (chip ^ slot))
            total = total + jnp.where(use, parts[k][...], 0.0)
    return total


def scan_a_kernel(*refs):
    parts, ahead, outs = refs[:4], refs[4:-4], refs[-4:]
    _, chip, _, even = place()
    for slot in range(4):
        start = ahead[0][...] if ahead else jnp.zeros((HEAD_DIM, HEAD_DIM), jnp.float32)
        outs[slot][...] = scan(parts, start, slot, chip, even)


def scan_b_kernel(*refs):
    scanned_a, parts, ahead, outs = refs[:4], refs[4:8], refs[8], refs[9:]
    _, chip, _, even = place()
    for slot in range(4):
        outs[slot][0] = scanned_a[slot][...]
        outs[slot][1] = scan(parts, ahead[...], slot, chip, jnp.logical_not(even))


def pair_kernel(slots, keep_a, keep_b, *refs):
    core, _, _, even = place()
    last = (core == 1) == even
    out = refs[-1]
    for n, slot in enumerate(slots):
        out[n, 0] = refs[n][0] + jnp.where(last, 0.0, keep_a[slot])
        out[n, 1] = refs[n][1] + jnp.where(last, keep_b[slot], 0.0)


def final_kernel(factor, half, k_ref, v_ref, g_ref, qi_ref, ki_ref, vi_ref, *refs):
    qo_hbm, ko_hbm, vo_hbm, buffer, sems = refs[-5:]
    core, chip, _, even = place()
    last = (core == 1) == even

    def total(slot, i):
        if half == 1:
            for ref, slots in zip(refs, PIECES):
                if slot in slots:
                    return ref[slots.index(slot), i].astype(jnp.bfloat16)
        use = last if i == 0 else jnp.logical_not(last)
        return (refs[slot][i] + jnp.where(use, refs[4 + i][slot], 0.0)).astype(jnp.bfloat16)

    stores = []
    for slot in (slot for slots in PIECES for slot in slots):
        cols = columns(half, slot, core, chip)
        a, b = total(slot, 0), total(slot, 1)
        earlier, future = jnp.where(even, a, b), jnp.where(even, b, a)
        qo = qi_ref[:, cols] + dot(g_ref[:, cols], earlier, ((1,), (1,)))
        ko = ki_ref[:, cols] + dot(v_ref[:, cols], future, ((1,), (1,)))
        vo = vi_ref[:, cols] + dot(k_ref[:, cols], future, ((1,), (0,)))
        for i, (value, out) in enumerate(((qo, qo_hbm), (ko, ko_hbm), (vo, vo_hbm))):
            buffer[i, slot] = (factor * value).astype(jnp.bfloat16)
            stores.append(pltpu.make_async_copy(buffer.at[i, slot], out.at[:, cols], sems.at[i, slot]))
            stores[-1].start()
    for store in stores:
        store.wait()


def final(factor, half, inputs, outs=()):
    out = jax.ShapeDtypeStruct(inputs[0].shape, jnp.bfloat16)
    return pl.pallas_call(
        lambda *refs: final_kernel(factor, half, *refs),
        out_shape=(out, out, out),
        in_specs=[VMEM] * len(inputs) + [HBM] * len(outs),
        out_specs=(HBM,) * 3,
        scratch_shapes=[pltpu.VMEM((3, 4, GROUP, HEAD_DIM), jnp.bfloat16), pltpu.SemaphoreType.DMA((3, 4))],
        input_output_aliases={len(inputs) + i: i for i in range(len(outs))},
        compiler_params=PARAMS,
        name="final",
    )(*inputs, *outs)


def between_squares(sum_a, sum_b, squares):
    if squares == 2:
        return [swap(sum_a, 8)]
    _, _, square, even = place()
    kv, qg = jnp.where(even, sum_a, sum_b), jnp.where(even, sum_b, sum_a)
    before, after = jnp.zeros_like(kv), jnp.zeros_like(qg)
    half = 1
    while half < squares:
        upper = (square & half) != 0
        out = jnp.where(upper, after + qg, before + kv)
        got = jnp.zeros_like(out)
        for step in range(half):
            pairs = []
            for base in range(0, squares, 2 * half):
                low, high = base + half - 1, base + half
                for r in range(8):
                    pairs.append((8 * low + r, 8 * (high + step) + r))
                    pairs.append((8 * high + r, 8 * (low - step) + r))
            got = got + lax.ppermute(out, AXIS, pairs)
        before, after = jnp.where(upper, before + got, before), jnp.where(upper, after, after + got)
        half *= 2
    return [jnp.where(even, before, after), jnp.where(even, after, before)]


def local(*args):
    devices = lax.axis_size(AXIS)
    factor = 1.0 / math.sqrt(HEAD_DIM * args[0].shape[0] * devices)

    *args, send_a = first_states(args)
    got_a = swap(send_a, 1)
    send_b, keep_a, keep_b = in_vmem(second_kernel, (heads(4),) * 3, args, "second_states")
    got_b = swap(send_b, 1)
    rows = jax.ShapeDtypeStruct(args[0].shape, jnp.float32)
    own_part = in_vmem(inner_kernel, (rows,) * 3, args, "inner")

    parts_a = [keep_a[0] + got_a[0]] + [swap(keep_a[m] + got_a[m], 2 * m) for m in (1, 2, 3)]
    parts_b = [keep_b[0] + got_b[0]] + [swap(keep_b[m] + got_b[m], 2 * m) for m in (1, 2, 3)]
    sum_a = parts_a[0]
    for m in (2, 3, 1):
        (sum_a,) = lax.optimization_barrier((sum_a + parts_a[m],))
    ahead = between_squares(sum_a, sum(parts_b[1:], parts_b[0]), devices // 8)
    scanned = in_vmem(scan_a_kernel, (heads(),) * 4, (*parts_a, *ahead[:-1]), "scan_a")
    scanned = in_vmem(scan_b_kernel, (heads(2),) * 4, (*scanned, *parts_b, ahead[-1]), "scan_b")
    back = [scanned[0]] + [swap(scanned[m], 2 * m) for m in (1, 2, 3)]
    back[1], own_part = lax.optimization_barrier((back[1], own_part))

    others = []
    for slots in PIECES:
        kernel = lambda *refs, slots=slots: pair_kernel(slots, *refs)
        pair = in_vmem(kernel, heads(len(slots), 2), (keep_a, keep_b, *(back[m] for m in slots)), "pair")
        others.append(swap(pair, 1))
    inputs = (*args[1:], *own_part)
    outs = final(factor, 0, (*inputs, *back, got_a, got_b))
    return final(factor, 1, (*inputs, *others), outs)


def solution(mesh):
    spec = P(("parts", "seq"), None)
    return jax.shard_map(local, mesh=mesh, in_specs=(spec,) * 4, out_specs=(spec,) * 3, check_vma=False)
```

```python
import math

import jax
import jax.numpy as jnp
from jax import lax
from jax.experimental import pallas as pl
from jax.experimental.pallas import tpu as pltpu
from jax.sharding import PartitionSpec as P

HEADS = 8
HEAD_DIM = 128
GROUP = 128
AXIS = "seq"
VMEM = pl.BlockSpec(memory_space=pltpu.VMEM)
HBM = pl.BlockSpec(memory_space=pltpu.HBM)
PARAMS = pltpu.CompilerParams(vmem_limit_bytes=16 * 2**20)
PIECES = ((0, 3), (1, 2))


def place():
    index = lax.axis_index(AXIS)
    square = index >> 3
    return index & 1, (index >> 1) & 3, square, (square & 1) == 0


def swap(x, mask):
    count = lax.axis_size(AXIS)
    return lax.ppermute(x, AXIS, [(i, i ^ mask) for i in range(count)])


def columns(half, slot, core, chip):
    return pl.ds(pl.multiple_of((4 * (core ^ half) + (chip ^ slot)) * HEAD_DIM, HEAD_DIM), HEAD_DIM)


def dot(a, b, dims):
    return lax.dot_general(a, b, (dims, ((), ())), preferred_element_type=jnp.float32)


def heads(*count):
    return jax.ShapeDtypeStruct((*count, HEAD_DIM, HEAD_DIM), jnp.float32)


def in_vmem(kernel, out_shape, args, name):
    return pl.pallas_call(
        kernel,
        out_shape=out_shape,
        in_specs=[VMEM] * len(args),
        out_specs=jax.tree.map(lambda _: VMEM, out_shape),
        compiler_params=PARAMS,
        name=name,
    )(*args)


def write_states(x_ref, y_ref, out_ref, half, core, chip):
    for slot in range(4):
        cols = columns(half, slot, core, chip)
        out_ref[slot] = dot(x_ref[:, cols], y_ref[:, cols], ((0,), (0,)))


def first_kernel(q_hbm, k_hbm, v_hbm, g_hbm, q_ref, k_ref, v_ref, g_ref, send_ref, sems):
    core, chip, _, even = place()
    q, k, v, g = (
        pltpu.make_async_copy(src, dst, sems.at[i])
        for i, (src, dst) in enumerate(((q_hbm, q_ref), (k_hbm, k_ref), (v_hbm, v_ref), (g_hbm, g_ref)))
    )

    def run(now, later, x_ref, y_ref):
        for load in (*now, *later):
            load.start()
        for load in now:
            load.wait()
        write_states(x_ref, y_ref, send_ref, 1, core, chip)
        for load in later:
            load.wait()

    pl.when(even)(lambda: run((k, v), (q, g), k_ref, v_ref))
    pl.when(jnp.logical_not(even))(lambda: run((q, g), (k, v), q_ref, g_ref))


def first_states(args):
    rows = jax.ShapeDtypeStruct(args[0].shape, args[0].dtype)
    return pl.pallas_call(
        first_kernel,
        out_shape=(rows,) * 4 + (heads(4),),
        in_specs=[HBM] * 4,
        out_specs=(VMEM,) * 5,
        scratch_shapes=[pltpu.SemaphoreType.DMA((4,))],
        compiler_params=PARAMS,
        name="first_states",
    )(*(pltpu.with_memory_space_constraint(x, pltpu.HBM) for x in args))


def second_kernel(q_ref, k_ref, v_ref, g_ref, send_b, keep_a, keep_b):
    core, chip, _, even = place()

    def run(x_ref, y_ref, z_ref, w_ref):
        write_states(z_ref, w_ref, send_b, 1, core, chip)
        write_states(x_ref, y_ref, keep_a, 0, core, chip)
        write_states(z_ref, w_ref, keep_b, 0, core, chip)

    pl.when(even)(lambda: run(k_ref, v_ref, q_ref, g_ref))
    pl.when(jnp.logical_not(even))(lambda: run(q_ref, g_ref, k_ref, v_ref))


def inner_kernel(q_ref, k_ref, v_ref, g_ref, qo_ref, ko_ref, vo_ref):
    row = lax.broadcasted_iota(jnp.int32, (GROUP, GROUP), 0)
    col = lax.broadcasted_iota(jnp.int32, (GROUP, GROUP), 1)
    causal = col <= row
    for head in range(HEADS):
        cols = slice(head * HEAD_DIM, (head + 1) * HEAD_DIM)
        q, k, v, g = q_ref[:, cols], k_ref[:, cols], v_ref[:, cols], g_ref[:, cols]
        scores = jnp.where(causal, dot(q, k, ((1,), (1,))), 0.0).astype(jnp.bfloat16)
        grads = jnp.where(causal, dot(g, v, ((1,), (1,))), 0.0).astype(jnp.bfloat16)
        qo_ref[:, cols] = dot(grads, k, ((1,), (0,)))
        ko_ref[:, cols] = dot(grads, q, ((0,), (0,)))
        vo_ref[:, cols] = dot(scores, g, ((0,), (0,)))


def scan(parts, start, slot, chip, forward):
    total = start
    for k in range(4):
        if k != slot:
            use = jnp.where(forward, (chip ^ k) < (chip ^ slot), (chip ^ k) > (chip ^ slot))
            total = total + jnp.where(use, parts[k][...], 0.0)
    return total


def sum_kernel(*refs):
    refs[4][...] = (refs[0][...] + refs[1][...]) + (refs[2][...] + refs[3][...])


def scan_a_kernel(*refs):
    parts, ahead, outs = refs[:4], refs[4:-4], refs[-4:]
    _, chip, _, even = place()
    for slot in range(4):
        start = ahead[0][...] if ahead else jnp.zeros((HEAD_DIM, HEAD_DIM), jnp.float32)
        outs[slot][...] = scan(parts, start, slot, chip, even)


def scan_b_kernel(*refs):
    scanned_a, ahead, outs = refs[:4], refs[8], refs[9:]
    parts = [refs[4 + n] for n in (0, 1, 2, 3)]
    _, chip, _, even = place()
    for slot in range(4):
        outs[slot][0] = scanned_a[slot][...]
        outs[slot][1] = scan(parts, ahead[...], slot, chip, jnp.logical_not(even))


def pair_kernel(slots, keep_a, keep_b, *refs):
    core, _, _, even = place()
    last = (core == 1) == even
    out = refs[-1]
    for n, slot in enumerate(slots):
        out[n, 0] = refs[n][0] + jnp.where(last, 0.0, keep_a[slot])
        out[n, 1] = refs[n][1] + jnp.where(last, keep_b[slot], 0.0)


def final_kernel(factor, work, k_ref, v_ref, g_ref, qi_ref, ki_ref, vi_ref, *refs):
    qo_hbm, ko_hbm, vo_hbm, buffer, sems = refs[-5:]
    core, chip, _, even = place()
    last = (core == 1) == even

    def total(half, slot, i):
        if half == 1:
            piece = [slot in slots for slots in PIECES].index(True)
            ref = refs[6] if piece == 0 else refs[0]
            return ref[PIECES[piece].index(slot), i].astype(jnp.bfloat16)
        use = last if i == 0 else jnp.logical_not(last)
        return (refs[slot][i] + jnp.where(use, refs[4 + i][slot], 0.0)).astype(jnp.bfloat16)

    stores = []
    for n, (half, slot) in enumerate(work):
        cols = columns(half, slot, core, chip)
        a, b = total(half, slot, 0), total(half, slot, 1)
        earlier, future = jnp.where(even, a, b), jnp.where(even, b, a)
        qo = qi_ref[:, cols] + dot(g_ref[:, cols], earlier, ((1,), (1,)))
        ko = ki_ref[:, cols] + dot(v_ref[:, cols], future, ((1,), (1,)))
        vo = vi_ref[:, cols] + dot(k_ref[:, cols], future, ((1,), (0,)))
        for i, (value, out) in enumerate(((qo, qo_hbm), (ko, ko_hbm), (vo, vo_hbm))):
            buffer[i, n] = (factor * value).astype(jnp.bfloat16)
            stores.append(pltpu.make_async_copy(buffer.at[i, n], out.at[:, cols], sems.at[i, n]))
            stores[-1].start()
    for store in stores:
        store.wait()


def final(factor, work, inputs, outs=()):
    out = jax.ShapeDtypeStruct(inputs[0].shape, jnp.bfloat16)
    return pl.pallas_call(
        lambda *refs: final_kernel(factor, work, *refs),
        out_shape=(out, out, out),
        in_specs=[VMEM] * len(inputs) + [HBM] * len(outs),
        out_specs=(HBM,) * 3,
        scratch_shapes=[
            pltpu.VMEM((3, len(work), GROUP, HEAD_DIM), jnp.bfloat16),
            pltpu.SemaphoreType.DMA((3, len(work))),
        ],
        input_output_aliases={len(inputs) + i: i for i in range(len(outs))},
        compiler_params=PARAMS,
        name="final",
    )(*inputs, *outs)


def between_squares(sum_a, sum_b, squares):
    if squares == 2:
        return [swap(sum_a, 8)]
    _, _, square, even = place()
    kv, qg = jnp.where(even, sum_a, sum_b), jnp.where(even, sum_b, sum_a)
    before, after = jnp.zeros_like(kv), jnp.zeros_like(qg)
    half = 1
    while half < squares:
        upper = (square & half) != 0
        out = jnp.where(upper, after + qg, before + kv)
        got = jnp.zeros_like(out)
        for step in range(half):
            pairs = []
            for base in range(0, squares, 2 * half):
                low, high = base + half - 1, base + half
                for r in range(8):
                    pairs.append((8 * low + r, 8 * (high + step) + r))
                    pairs.append((8 * high + r, 8 * (low - step) + r))
            got = got + lax.ppermute(out, AXIS, pairs)
        before, after = jnp.where(upper, before + got, before), jnp.where(upper, after, after + got)
        half *= 2
    return [jnp.where(even, before, after), jnp.where(even, after, before)]


def local(*args):
    devices = lax.axis_size(AXIS)
    assert args[0].shape[0] == GROUP and devices % 8 == 0
    factor = 1.0 / math.sqrt(HEAD_DIM * args[0].shape[0] * devices)

    *args, send_a = first_states(args)
    got_a = swap(send_a, 1)
    send_b, keep_a, keep_b = in_vmem(second_kernel, (heads(4),) * 3, args, "second_states")
    got_b = swap(send_b, 1)
    rows = jax.ShapeDtypeStruct(args[0].shape, jnp.float32)
    own_part = in_vmem(inner_kernel, (rows,) * 3, args, "inner")

    parts_a = [keep_a[0] + got_a[0]] + [swap(keep_a[m] + got_a[m], 2 * m) for m in (1, 2, 3)]
    parts_b = [keep_b[0] + got_b[0]] + [swap(keep_b[m] + got_b[m], 2 * m) for m in (1, 2, 3)]
    sum_a = in_vmem(sum_kernel, heads(), [parts_a[m] for m in (0, 3, 2, 1)], "sum_a")
    ahead = between_squares(sum_a, sum(parts_b[1:], parts_b[0]), devices // 8)
    scanned = in_vmem(scan_a_kernel, (heads(),) * 4, (*parts_a, *ahead[:-1]), "scan_a")
    scanned = in_vmem(scan_b_kernel, (heads(2),) * 4, (*scanned, *(parts_b[m] for m in (0, 1, 2, 3)), ahead[-1]), "scan_b")
    back = [scanned[0]] + [swap(scanned[m], 2 * m) for m in (1, 2, 3)]
    back[1], own_part = lax.optimization_barrier((back[1], own_part))

    others = []
    for slots in PIECES:
        kernel = lambda *refs, slots=slots: pair_kernel(slots, *refs)
        pair = in_vmem(kernel, heads(len(slots), 2), (keep_a, keep_b, *(back[m] for m in slots)), "pair")
        others.append(swap(pair, 1))
    inputs = (*args[1:], *own_part)
    work = [(0, slot) for slots in PIECES for slot in slots] + [(1, slot) for slot in PIECES[0]]
    outs = final(factor, work, (*inputs, *back, got_a, got_b, others[0]))
    return final(factor, [(1, slot) for slot in PIECES[1]], (*inputs, others[1]), outs)


def solution(mesh):
    spec = P(("parts", "seq"), None)
    return jax.shard_map(local, mesh=mesh, in_specs=(spec,) * 4, out_specs=(spec,) * 3, check_vma=False)
```

```python
import math

import jax
import jax.numpy as jnp
from jax import lax
from jax.experimental import pallas as pl
from jax.experimental.pallas import tpu as pltpu
from jax.sharding import PartitionSpec as P

HEADS = 8
HEAD_DIM = 128
GROUP = 128
AXIS = "seq"
VMEM = pl.BlockSpec(memory_space=pltpu.VMEM)
HBM = pl.BlockSpec(memory_space=pltpu.HBM)
PARAMS = pltpu.CompilerParams(vmem_limit_bytes=16 * 2**20)
PIECES = ((0, 1), (2, 3))


def place():
    index = lax.axis_index(AXIS)
    square = index >> 3
    return index & 1, (index >> 1) & 3, square, (square & 1) == 0


def swap(x, mask):
    count = lax.axis_size(AXIS)
    return lax.ppermute(x, AXIS, [(i, i ^ mask) for i in range(count)])


def columns(half, slot, core, chip):
    return pl.ds(pl.multiple_of((4 * (core ^ half) + (chip ^ slot)) * HEAD_DIM, HEAD_DIM), HEAD_DIM)


def dot(a, b, dims):
    return lax.dot_general(a, b, (dims, ((), ())), preferred_element_type=jnp.float32)


def heads(*count):
    return jax.ShapeDtypeStruct((*count, HEAD_DIM, HEAD_DIM), jnp.float32)


def in_vmem(kernel, out_shape, args, name):
    return pl.pallas_call(
        kernel,
        out_shape=out_shape,
        in_specs=[VMEM] * len(args),
        out_specs=jax.tree.map(lambda _: VMEM, out_shape),
        compiler_params=PARAMS,
        name=name,
    )(*args)


def write_states(x_ref, y_ref, out_ref, half, core, chip):
    for slot in range(4):
        cols = columns(half, slot, core, chip)
        out_ref[slot] = dot(x_ref[:, cols], y_ref[:, cols], ((0,), (0,)))


def first_kernel(q_hbm, k_hbm, v_hbm, g_hbm, q_ref, k_ref, v_ref, g_ref, send_ref, sems):
    core, chip, _, even = place()
    q, k, v, g = (
        pltpu.make_async_copy(src, dst, sems.at[i])
        for i, (src, dst) in enumerate(((q_hbm, q_ref), (k_hbm, k_ref), (v_hbm, v_ref), (g_hbm, g_ref)))
    )

    def run(now, later, x_ref, y_ref):
        for load in (*now, *later):
            load.start()
        for load in now:
            load.wait()
        write_states(x_ref, y_ref, send_ref, 1, core, chip)
        for load in later:
            load.wait()

    pl.when(even)(lambda: run((k, v), (q, g), k_ref, v_ref))
    pl.when(jnp.logical_not(even))(lambda: run((q, g), (k, v), q_ref, g_ref))


def first_states(args):
    rows = jax.ShapeDtypeStruct(args[0].shape, args[0].dtype)
    return pl.pallas_call(
        first_kernel,
        out_shape=(rows,) * 4 + (heads(4),),
        in_specs=[HBM] * 4,
        out_specs=(VMEM,) * 5,
        scratch_shapes=[pltpu.SemaphoreType.DMA((4,))],
        compiler_params=PARAMS,
        name="first_states",
    )(*(pltpu.with_memory_space_constraint(x, pltpu.HBM) for x in args))


def second_kernel(q_ref, k_ref, v_ref, g_ref, send_b, keep_a, keep_b):
    core, chip, _, even = place()

    def run(x_ref, y_ref, z_ref, w_ref):
        write_states(z_ref, w_ref, send_b, 1, core, chip)
        write_states(x_ref, y_ref, keep_a, 0, core, chip)
        write_states(z_ref, w_ref, keep_b, 0, core, chip)

    pl.when(even)(lambda: run(k_ref, v_ref, q_ref, g_ref))
    pl.when(jnp.logical_not(even))(lambda: run(q_ref, g_ref, k_ref, v_ref))


def inner_kernel(q_ref, k_ref, v_ref, g_ref, qo_ref, ko_ref, vo_ref):
    row = lax.broadcasted_iota(jnp.int32, (GROUP, GROUP), 0)
    col = lax.broadcasted_iota(jnp.int32, (GROUP, GROUP), 1)
    causal = col <= row
    for head in range(HEADS):
        cols = slice(head * HEAD_DIM, (head + 1) * HEAD_DIM)
        q, k, v, g = q_ref[:, cols], k_ref[:, cols], v_ref[:, cols], g_ref[:, cols]
        scores = jnp.where(causal, dot(q, k, ((1,), (1,))), 0.0).astype(jnp.bfloat16)
        grads = jnp.where(causal, dot(g, v, ((1,), (1,))), 0.0).astype(jnp.bfloat16)
        qo_ref[:, cols] = dot(grads, k, ((1,), (0,)))
        ko_ref[:, cols] = dot(grads, q, ((0,), (0,)))
        vo_ref[:, cols] = dot(scores, g, ((0,), (0,)))


def scan(parts, start, slot, chip, forward):
    total = start
    for k in range(4):
        if k != slot:
            use = jnp.where(forward, (chip ^ k) < (chip ^ slot), (chip ^ k) > (chip ^ slot))
            total = total + jnp.where(use, parts[k][...], 0.0)
    return total


def sum_kernel(*refs):
    refs[4][...] = (refs[0][...] + refs[1][...]) + (refs[2][...] + refs[3][...])


def scan_a_kernel(*refs):
    parts, ahead, outs = refs[:4], refs[4:-4], refs[-4:]
    _, chip, _, even = place()
    for slot in range(4):
        start = ahead[0][...] if ahead else jnp.zeros((HEAD_DIM, HEAD_DIM), jnp.float32)
        outs[slot][...] = scan(parts, start, slot, chip, even)


def scan_b_kernel(*refs):
    scanned_a, ahead, outs = refs[:4], refs[8], refs[9:]
    parts = [refs[4 + n] for n in (0, 3, 1, 2)]
    _, chip, _, even = place()
    for slot in range(4):
        outs[slot][0] = scanned_a[slot][...]
        outs[slot][1] = scan(parts, ahead[...], slot, chip, jnp.logical_not(even))


def pair_kernel(slots, keep_a, keep_b, *refs):
    core, _, _, even = place()
    last = (core == 1) == even
    out = refs[-1]
    for n, slot in enumerate(slots):
        out[n, 0] = refs[n][0] + jnp.where(last, 0.0, keep_a[slot])
        out[n, 1] = refs[n][1] + jnp.where(last, keep_b[slot], 0.0)


def final_kernel(factor, work, k_ref, v_ref, g_ref, qi_ref, ki_ref, vi_ref, *refs):
    qo_hbm, ko_hbm, vo_hbm, buffer, sems = refs[-5:]
    core, chip, _, even = place()
    last = (core == 1) == even

    def total(half, slot, i):
        if half == 1:
            piece = [slot in slots for slots in PIECES].index(True)
            ref = refs[6] if piece == 0 else refs[0]
            return ref[PIECES[piece].index(slot), i].astype(jnp.bfloat16)
        use = last if i == 0 else jnp.logical_not(last)
        return (refs[slot][i] + jnp.where(use, refs[4 + i][slot], 0.0)).astype(jnp.bfloat16)

    stores = []
    for n, (half, slot) in enumerate(work):
        cols = columns(half, slot, core, chip)
        a, b = total(half, slot, 0), total(half, slot, 1)
        earlier, future = jnp.where(even, a, b), jnp.where(even, b, a)
        qo = qi_ref[:, cols] + dot(g_ref[:, cols], earlier, ((1,), (1,)))
        ko = ki_ref[:, cols] + dot(v_ref[:, cols], future, ((1,), (1,)))
        vo = vi_ref[:, cols] + dot(k_ref[:, cols], future, ((1,), (0,)))
        for i, (value, out) in enumerate(((qo, qo_hbm), (ko, ko_hbm), (vo, vo_hbm))):
            buffer[i, n] = (factor * value).astype(jnp.bfloat16)
            stores.append(pltpu.make_async_copy(buffer.at[i, n], out.at[:, cols], sems.at[i, n]))
            stores[-1].start()
    for store in stores:
        store.wait()


def final(factor, work, inputs, outs=()):
    out = jax.ShapeDtypeStruct(inputs[0].shape, jnp.bfloat16)
    return pl.pallas_call(
        lambda *refs: final_kernel(factor, work, *refs),
        out_shape=(out, out, out),
        in_specs=[VMEM] * len(inputs) + [HBM] * len(outs),
        out_specs=(HBM,) * 3,
        scratch_shapes=[
            pltpu.VMEM((3, len(work), GROUP, HEAD_DIM), jnp.bfloat16),
            pltpu.SemaphoreType.DMA((3, len(work))),
        ],
        input_output_aliases={len(inputs) + i: i for i in range(len(outs))},
        compiler_params=PARAMS,
        name="final",
    )(*inputs, *outs)


def between_squares(sum_a, sum_b, squares):
    if squares == 2:
        return [swap(sum_a, 8)]
    _, _, square, even = place()
    kv, qg = jnp.where(even, sum_a, sum_b), jnp.where(even, sum_b, sum_a)
    before, after = jnp.zeros_like(kv), jnp.zeros_like(qg)
    half = 1
    while half < squares:
        upper = (square & half) != 0
        out = jnp.where(upper, after + qg, before + kv)
        got = jnp.zeros_like(out)
        for step in range(half):
            pairs = []
            for base in range(0, squares, 2 * half):
                low, high = base + half - 1, base + half
                for r in range(8):
                    pairs.append((8 * low + r, 8 * (high + step) + r))
                    pairs.append((8 * high + r, 8 * (low - step) + r))
            got = got + lax.ppermute(out, AXIS, pairs)
        before, after = jnp.where(upper, before + got, before), jnp.where(upper, after, after + got)
        half *= 2
    return [jnp.where(even, before, after), jnp.where(even, after, before)]


def local(*args):
    devices = lax.axis_size(AXIS)
    assert args[0].shape[0] == GROUP and devices % 8 == 0
    factor = 1.0 / math.sqrt(HEAD_DIM * args[0].shape[0] * devices)

    *args, send_a = first_states(args)
    got_a = swap(send_a, 1)
    send_b, keep_a, keep_b = in_vmem(second_kernel, (heads(4),) * 3, args, "second_states")
    got_b = swap(send_b, 1)
    rows = jax.ShapeDtypeStruct(args[0].shape, jnp.float32)
    own_part = in_vmem(inner_kernel, (rows,) * 3, args, "inner")

    parts_a = [keep_a[0] + got_a[0]] + [swap(keep_a[m] + got_a[m], 2 * m) for m in (1, 2, 3)]
    parts_b = [keep_b[0] + got_b[0]] + [swap(keep_b[m] + got_b[m], 2 * m) for m in (1, 2, 3)]
    sum_a = in_vmem(sum_kernel, heads(), [parts_a[m] for m in (0, 2, 3, 1)], "sum_a")
    ahead = between_squares(sum_a, sum(parts_b[1:], parts_b[0]), devices // 8)
    scanned = in_vmem(scan_a_kernel, (heads(),) * 4, (*parts_a, *ahead[:-1]), "scan_a")
    scanned = in_vmem(scan_b_kernel, (heads(2),) * 4, (*scanned, *(parts_b[m] for m in (0, 2, 3, 1)), ahead[-1]), "scan_b")
    back = [scanned[0]] + [swap(scanned[m], 2 * m) for m in (1, 2, 3)]
    back[3], own_part = lax.optimization_barrier((back[3], own_part))

    others = []
    for slots in PIECES:
        kernel = lambda *refs, slots=slots: pair_kernel(slots, *refs)
        pair = in_vmem(kernel, heads(len(slots), 2), (keep_a, keep_b, *(back[m] for m in slots)), "pair")
        others.append(swap(pair, 1))
    inputs = (*args[1:], *own_part)
    work = [(0, slot) for slots in PIECES for slot in slots] + [(1, slot) for slot in PIECES[0]]
    outs = final(factor, work, (*inputs, *back, got_a, got_b, others[0]))
    return final(factor, [(1, slot) for slot in PIECES[1]], (*inputs, others[1]), outs)


def solution(mesh):
    spec = P(("parts", "seq"), None)
    return jax.shard_map(local, mesh=mesh, in_specs=(spec,) * 4, out_specs=(spec,) * 3, check_vma=False)
```
